32 devices in a mesh: req: 8 (over z, x), mlp: 4 (over y, core).
Axes of the slice: x: 2, y: 2, z: 4, core: 2. Of those that a mesh axis runs over, the one named last changes fastest.
Arguments:
- tokens: bfloat16 [16384, 1024], P(('req', 'mlp')), may hold values from -72 to 72
- attend_weight: bfloat16 [1024, 3072], replicated, may hold values from -0.1875 to 0.1875
- output_weight: bfloat16 [1024, 1024], replicated, may hold values from -0.1875 to 0.1875
- attend_gain: float32 [1024], replicated, may hold values from 0.1 to 1.9
- up_weight: bfloat16 [1024, 4096], P(None, 'mlp'), may hold values from -0.1875 to 0.1875
- down_weight: bfloat16 [1024, 4096], P(None, 'mlp'), may hold values from -0.09375 to 0.09375
- mlp_gain: float32 [1024], replicated, may hold values from 0.1 to 1.9
- embed_weight: bfloat16 [1024, 128], replicated, may hold values from -0.1875 to 0.1875
- query_length: int32 [128], P(('req', 'mlp')), may hold values from 1 to 128, 12288 in all
- documents: bfloat16 [64, 256, 128], P('req', 'mlp'), may hold values from -0.54 to 0.54
- document_length: int32 [64], P('req'), may hold values from 1 to 256, 8256 in all
- candidates: int32 [128, 8], P(('req', 'mlp')), may hold values from 0 to 63
Outputs:
- embedded: bfloat16 [16384, 128], P(('req', 'mlp'))
- scores: float32 [128, 8], P(('req', 'mlp'))
The draws below stay inside these ranges and needn't reach their ends.
All inputs are finite; a program needn't handle non-finite values. No bound on the sum of `query_length` or of `document_length` on one device may be relied on, other than what follows from the above.
Results may differ from the reference program's by a relative error of at most 0.015.
The reference program's roundings to bfloat16 on the way (of `packed`, `probs`, `context`, `normed`, `inner` and `layer_out`) count: a program that leaves them out, or rounds other values in their place, can miss the bound.
Values may be sent and summed in bfloat16 or wider, within the bound.
A program may use at most 128 MiB of HBM per device.

```python
import math
import jax
import jax.numpy as jnp
import numpy as np
from jax import lax

D = 1024
HEADS = 16
HD = 64
FF = 4096
P_SIZE = 128
SEQ = 128
DLEN = 256
CAND = 8
REQS = 128
TOKENS = 16384
DOCS = 64


def draw_tokens(key, part):
    noise_key = jax.random.fold_in(key, 11)
    topic_key = jax.random.fold_in(key, 13)
    groups = TOKENS // SEQ
    noise = jax.random.truncated_normal(noise_key, -3.0, 3.0, (groups, SEQ, D), jnp.float32)
    topic = jax.random.truncated_normal(topic_key, -3.0, 3.0, (groups, 1, D), jnp.float32)
    base = (noise + topic).reshape(TOKENS, D)
    return base.astype(jnp.bfloat16)


def draw_documents(key, part):
    noise_key = jax.random.fold_in(key, 21)
    head_key = jax.random.fold_in(key, 23)
    tail_key = jax.random.fold_in(key, 29)
    noise = 0.08 * jax.random.truncated_normal(noise_key, -6.0, 6.0, (DOCS, DLEN, P_SIZE), jnp.float32)
    weight_topic = 2.0 / math.sqrt(P_SIZE)
    head = jnp.where(jax.random.bernoulli(head_key, 0.5, (DOCS, 1, P_SIZE)), weight_topic, -weight_topic)
    tail = jnp.where(jax.random.bernoulli(tail_key, 0.5, (DOCS, 1, P_SIZE)), weight_topic, -weight_topic)
    late = (jnp.arange(DLEN) >= DLEN * 3 // 4)[None, :, None]
    topic = jnp.where(late, tail, head)
    return jnp.clip(noise + topic, -0.54, 0.54).astype(jnp.bfloat16)


def touch_ends(result, key, least, largest):
    longest = result.shape.index(max(result.shape))
    spots = []
    for shift in (0, 1):
        where = [jax.random.randint(jax.random.fold_in(key, axis), (), 0, length) for axis, length in enumerate(result.shape)]
        where[longest] = (where[longest] + shift) % result.shape[longest]
        spots.append(tuple(where))
    return result.at[spots[0]].set(least).at[spots[1]].set(largest)


def shard_levels(stream_key, shape, pieces, low, top_value):
    def one(dim, parts):
        heights = jax.random.uniform(jax.random.fold_in(jax.random.fold_in(stream_key, 6), dim), (parts,), jnp.float32, low / len(pieces), top_value / len(pieces))
        return jnp.repeat(jnp.exp(heights), shape[dim] // parts).reshape((-1,) + (1,) * (len(shape) - dim - 1))

    loudness = one(*pieces[0])
    for cut in pieces[1:]:
        loudness = loudness * one(*cut)
    return loudness


def rank_table(amount, skew):
    portions = [(1 << 20) // math.isqrt(rank ** skew) + 1 for rank in range(1, amount + 1)]
    width = 1 + sum(portions) // (1 << 30)
    return np.cumsum(np.array([max(1, weight // width) for weight in portions]))


def skewed_ids(stream_key, extent, count, lean):
    listing = rank_table(count, lean)
    pick = jax.random.randint(jax.random.fold_in(stream_key, 1), extent, 0, int(listing[count - 1]))
    rank = jnp.searchsorted(jnp.asarray(listing, jnp.int32), pick, side="right")
    return jax.random.permutation(jax.random.fold_in(stream_key, 2), count)[rank].astype(jnp.int32)


def length_profile(number_of, total, most, skew):
    portions = [(1 << 20) // math.isqrt(rank ** skew) + 1 for rank in range(2, number_of + 1)]
    surplus, holding = total - most - (number_of - 1), [1] * (number_of - 1)
    while surplus > 0:
        free = [i for i in range(number_of - 1) if holding[i] < most]
        mass, budget = sum([portions[i] for i in free]), surplus
        for i in free:
            addition = min(most - holding[i], max(1, budget * portions[i] // mass), surplus)
            holding[i] = holding[i] + addition
            surplus = surplus - addition
    return np.array([most] + holding)


def ragged(key, count, total, reach, slope):
    if count == 2:
        one = jax.random.randint(key, (), max(1, total - reach), min(reach, total - 1) + 1)
        return jnp.stack([one, total - one])
    sizes = jnp.asarray(length_profile(count, total, reach, slope), jnp.int32)
    twos = (count - 1) // 2
    giver, receiver = sizes[1:1 + 2 * twos:2], sizes[2:2 + 2 * twos:2]
    slack = jnp.minimum(giver - 1, reach - receiver)
    shifted = jax.random.randint(jax.random.fold_in(key, 1), (twos,), 0, 1 << 20) % (slack + 1)
    sizes = sizes.at[1:1 + 2 * twos:2].set(giver - shifted).at[2:2 + 2 * twos:2].set(receiver + shifted)
    return sizes[jax.random.permutation(jax.random.fold_in(key, 2), count)]


def normal_values(rng, extent, deviation, reach, shards=(), held_as=jnp.bfloat16):
    values = deviation * jax.random.normal(rng, extent, jnp.float32)
    if shards:
        values = values * shard_levels(rng, extent, shards, -0.22, 0.18)
    return jnp.clip(values, -reach, reach).astype(held_as)


def setup_inputs(seed: int = 0) -> dict:
    arg_keys = jax.random.split(jax.random.key(seed), 13)
    tokens = draw_tokens(jax.random.fold_in(arg_keys[12], 71), 0)
    attend_weight = normal_values(arg_keys[1], (D, 3 * D), D ** -0.5, 0.1875)
    output_weight = normal_values(arg_keys[2], (D, D), D ** -0.5, 0.1875)
    attend_gain = jnp.clip(1.0 + 0.18 * jax.random.normal(arg_keys[3], (D,), jnp.float32), 0.1, 1.9)
    up_weight = normal_values(arg_keys[4], (D, FF), D ** -0.5, 0.1875, ((1, 4),))
    down_weight = normal_values(arg_keys[5], (D, FF), FF ** -0.5, 0.09375, ((1, 4),))
    mlp_gain = jnp.clip(1.0 + 0.18 * jax.random.normal(arg_keys[6], (D,), jnp.float32), 0.1, 1.9)
    embed_weight = normal_values(arg_keys[7], (D, P_SIZE), D ** -0.5, 0.1875)
    query_length = ragged(arg_keys[8], REQS, REQS * SEQ * 3 // 4, SEQ, 1).astype(jnp.int32)
    documents = draw_documents(jax.random.fold_in(arg_keys[12], 71), 0)
    document_length = ragged(arg_keys[10], DOCS, DOCS * DLEN // 2 + DOCS, DLEN, 1).astype(jnp.int32)
    candidates = touch_ends(skewed_ids(arg_keys[11], (REQS, CAND), DOCS, 2), jax.random.fold_in(arg_keys[11], 3), 0, DOCS - 1).astype(jnp.int32)
    return {"tokens": tokens, "attend_weight": attend_weight, "output_weight": output_weight, "attend_gain": attend_gain, "up_weight": up_weight, "down_weight": down_weight, "mlp_gain": mlp_gain, "embed_weight": embed_weight, "query_length": query_length, "documents": documents, "document_length": document_length, "candidates": candidates}


def norm_rows(values, scaling):
    average = lax.optimization_barrier(jnp.mean(values, axis=-1, keepdims=True))
    centred = values - average
    variance = lax.optimization_barrier(jnp.mean(centred * centred, axis=-1, keepdims=True))
    return centred * lax.rsqrt(variance + 1e-05) * scaling.astype(jnp.float32)

def reference(tokens, attend_weight, output_weight, attend_gain, up_weight, down_weight, mlp_gain, embed_weight, query_length, documents, document_length, candidates):
    rows = tokens.shape[0]
    requests = query_length.shape[0]
    packed = jnp.dot(tokens, attend_weight, preferred_element_type=jnp.float32).astype(jnp.bfloat16)
    packed = packed.reshape(requests, SEQ, 3, HEADS, HD).astype(jnp.float32)
    live_slot = jnp.arange(SEQ)[None, :] < query_length[:, None]
    logits = jnp.einsum('rqhd,rkhd->rhqk', packed[:, :, 0], packed[:, :, 1]) * HD ** (-0.5)
    logits = jnp.where(live_slot[:, None, None, :], logits, -1e+30)
    highest = lax.optimization_barrier(jnp.max(logits, axis=-1, keepdims=True))
    weights = jnp.exp(logits - highest)
    probs = (weights / lax.optimization_barrier(jnp.sum(weights, axis=-1, keepdims=True))).astype(jnp.bfloat16)
    context = jnp.einsum('rhqk,rkhd->rqhd', probs.astype(jnp.float32), packed[:, :, 2])
    context = context.astype(jnp.bfloat16).reshape(rows, D)
    attended = jnp.dot(context, output_weight, preferred_element_type=jnp.float32)
    normed = norm_rows(tokens.astype(jnp.float32) + attended, attend_gain).astype(jnp.bfloat16)
    inner = jax.nn.gelu(jnp.dot(normed, up_weight, preferred_element_type=jnp.float32), approximate=False).astype(jnp.bfloat16)
    reduced = jnp.dot(inner, down_weight.T, preferred_element_type=jnp.float32)
    layer_out = norm_rows(normed.astype(jnp.float32) + reduced, mlp_gain).astype(jnp.bfloat16)
    projected = jnp.dot(layer_out, embed_weight, preferred_element_type=jnp.float32)
    unit = projected * lax.rsqrt(lax.optimization_barrier(jnp.sum(projected * projected, axis=-1, keepdims=True)) + 1e-06)
    embedded = jnp.where(live_slot.reshape(rows, 1), unit, 0.0).astype(jnp.bfloat16)

    def score_one(item):
        block, picks = item
        chosen = documents[picks].astype(jnp.float32)
        limits = document_length[picks]
        sims = jnp.einsum('sp,ctp->sct', block.astype(jnp.float32), chosen)
        live_doc = jnp.arange(DLEN)[None, :] < limits[:, None]
        sims = jnp.where(live_doc[None], sims, -1e+30)
        return lax.optimization_barrier(jnp.sum(lax.optimization_barrier(jnp.max(sims, axis=2)), axis=0))
    scores = lax.map(score_one, (embedded.reshape(requests, SEQ, P_SIZE), candidates))
    return (embedded, scores)
```

```python
import functools

import jax
import jax.numpy as jnp
from jax import lax
from jax.experimental import pallas as pl
from jax.experimental.pallas import tpu as pltpu
from jax.sharding import PartitionSpec as P

D = 1024
HEADS = 16
HD = 64
P_SIZE = 128
SEQ = 128
CORES = 2
DEPTH = 4
MIB = 1024 * 1024


def norm_rows(values, scaling):
    average = jnp.mean(values, axis=-1, keepdims=True)
    centred = values - average
    variance = jnp.mean(centred * centred, axis=-1, keepdims=True)
    return centred * lax.rsqrt(variance + 1e-05) * scaling


def attend_kernel(length_ref, tokens_ref, attend_ref, output_ref, gain_ref, normed_ref, packed, context):
    rows = tokens_ref.shape[0]
    wide = 512

    def project(step, carry):
        columns = pl.ds(pl.multiple_of(step * wide, wide), wide)
        packed[:, columns] = jnp.dot(
            tokens_ref[...], attend_ref[:, columns], preferred_element_type=jnp.float32
        ).astype(jnp.bfloat16)
        return carry

    lax.fori_loop(0, 3 * D // wide, project, 0)
    lane = lax.broadcasted_iota(jnp.int32, (SEQ, 2 * HD), 1)
    low = lane < HD
    key_slot = lax.broadcasted_iota(jnp.int32, (2 * SEQ, SEQ), 1)

    def one_request(request, carry):
        here = pl.ds(pl.multiple_of(request * SEQ, SEQ), SEQ)
        live = key_slot < length_ref[request]
        for pair in range(HEADS // 2):
            at = pair * 2 * HD
            query = packed[here, at : at + 2 * HD]
            keys = packed[here, D + at : D + at + 2 * HD]
            value = packed[here, 2 * D + at : 2 * D + at + 2 * HD]
            none = jnp.zeros_like(query)
            both = jnp.concatenate([jnp.where(low, query, none), jnp.where(low, none, query)], axis=0)
            logits = lax.dot_general(
                both, keys, (((1,), (1,)), ((), ())), preferred_element_type=jnp.float32
            ) * HD ** (-0.5)
            logits = jnp.where(live, logits, -1e30)
            weights = jnp.exp(logits - jnp.max(logits, axis=-1, keepdims=True))
            probs = (weights / jnp.sum(weights, axis=-1, keepdims=True)).astype(jnp.bfloat16)
            mixed = jnp.dot(probs, value, preferred_element_type=jnp.float32)
            context[here, at : at + 2 * HD] = jnp.where(low, mixed[:SEQ], mixed[SEQ:]).astype(jnp.bfloat16)
        return carry

    lax.fori_loop(0, rows // SEQ, one_request, 0)

    def finish(step, carry):
        here = pl.ds(pl.multiple_of(step * SEQ, SEQ), SEQ)
        attended = jnp.dot(context[here, :], output_ref[...], preferred_element_type=jnp.float32)
        normed_ref[here, :] = norm_rows(
            tokens_ref[here, :].astype(jnp.float32) + attended, gain_ref[...]
        ).astype(jnp.bfloat16)
        return carry

    lax.fori_loop(0, rows // SEQ, finish, 0)


def attend(tokens, attend_weight, output_weight, attend_gain, query_length):
    rows = tokens.shape[0]
    vmem = pl.BlockSpec(memory_space=pltpu.VMEM)
    return pl.pallas_call(
        attend_kernel,
        out_shape=jax.ShapeDtypeStruct((rows, D), jnp.bfloat16),
        in_specs=[pl.BlockSpec(memory_space=pltpu.SMEM), vmem, vmem, vmem, vmem],
        out_specs=vmem,
        scratch_shapes=[pltpu.VMEM((rows, 3 * D), jnp.bfloat16), pltpu.VMEM((rows, D), jnp.bfloat16)],
        compiler_params=pltpu.CompilerParams(vmem_limit_bytes=32 * MIB),
        cost_estimate=pl.CostEstimate(flops=rows * D * D * 9, bytes_accessed=10 * MIB, transcendentals=rows * SEQ * HEADS),
        name="attend",
    )(query_length, tokens, attend_weight, output_weight, attend_gain.reshape(1, D))


def score_kernel(spots_ref, limits_ref, embedded_ref, pieces_ref, best_ref):
    requests, picks, parts = spots_ref.shape
    piece_rows = pieces_ref.shape[1]
    position = lax.broadcasted_iota(jnp.int32, (parts * piece_rows, SEQ), 0)

    def one_request(request, carry):
        block = embedded_ref[pl.ds(pl.multiple_of(request * SEQ, SEQ), SEQ), :]
        found = []
        for pick in range(picks):
            chosen = jnp.concatenate([pieces_ref[spots_ref[request, pick, part]] for part in range(parts)], axis=0)
            sims = lax.dot_general(
                chosen, block, (((1,), (1,)), ((), ())), preferred_element_type=jnp.float32
            )
            sims = jnp.where(position < limits_ref[request, pick], sims, -1e30)
            found.append(jnp.max(sims, axis=0, keepdims=True))
        best_ref[request] = jnp.concatenate(found, axis=0)
        return carry

    lax.fori_loop(0, requests, one_request, 0)


def score(embedded, pieces, spots, limits):
    requests, picks, parts = spots.shape
    smem, vmem = pl.BlockSpec(memory_space=pltpu.SMEM), pl.BlockSpec(memory_space=pltpu.VMEM)
    best = pl.pallas_call(
        score_kernel,
        out_shape=jax.ShapeDtypeStruct((requests, picks, SEQ), jnp.float32),
        in_specs=[smem, smem, vmem, vmem],
        out_specs=vmem,
        compiler_params=pltpu.CompilerParams(vmem_limit_bytes=32 * MIB),
        cost_estimate=pl.CostEstimate(flops=2 * requests * picks * 256 * SEQ * P_SIZE, bytes_accessed=5 * MIB, transcendentals=0),
        name="score",
    )(spots, limits, embedded, pieces)
    return jnp.sum(best, axis=2)


def on_device(
    req_size,
    mlp_size,
    tokens,
    attend_weight,
    output_weight,
    attend_gain,
    up_weight,
    down_weight,
    mlp_gain,
    embed_weight,
    query_length,
    documents,
    document_length,
    candidates,
):
    rows = tokens.shape[0]
    held_docs, shard_rows = documents.shape[:2]
    width, tall = req_size // DEPTH, mlp_size // CORES
    req, mlp = lax.axis_index("req"), lax.axis_index("mlp")
    z, x, y, core = req // width, req % width, mlp // CORES, mlp % CORES

    def to_core(block):
        return lax.ppermute(block, "mlp", [(m, m ^ 1) for m in range(mlp_size)])

    def along_y(block, hops):
        return lax.ppermute(block, "mlp", [(m, (m + CORES * hops) % mlp_size) for m in range(mlp_size)])

    def along_x(block, hops):
        return lax.ppermute(
            block, "req", [(r, r // width * width + (r % width + hops) % width) for r in range(req_size)]
        )

    def to_pair(block, stride):
        return lax.ppermute(block, "req", [(r, r ^ stride) for r in range(req_size)])

    around = jnp.stack([documents] + [along_y(documents, hop) for hop in range(1, tall)])
    around = jnp.stack([around] + [along_x(around, hop) for hop in range(1, width)])
    upward, downward = [around], [around]
    for _ in range(1, DEPTH):
        upward.append(lax.ppermute(upward[-1], "req", [(r, r + width) for r in range(req_size - width)]))
        downward.append(lax.ppermute(downward[-1], "req", [(r, r - width) for r in range(width, req_size)]))
    around = jnp.stack(
        [around] + [jnp.where(z >= hop, upward[hop], downward[DEPTH - hop]) for hop in range(1, DEPTH)]
    )
    pieces = jnp.stack([around, to_core(around)]).reshape(-1, shard_rows, P_SIZE)

    place = x % 2 + 2 * (z % 2)
    part_columns = up_weight.shape[1] // 4

    def part(weight, which):
        return lax.dynamic_slice_in_dim(weight, which * part_columns, part_columns, 1)

    own = [(up_weight, to_core(up_weight)), (down_weight, to_core(down_weight))]
    brought = [[], []]
    for hop in range(1, tall):
        for kind, weight in enumerate((up_weight, down_weight)):
            first = along_y(part(weight, place), hop)
            brought[kind] += [first, to_pair(first, 1), to_pair(first, width)]
        for kind, weight in enumerate((up_weight, down_weight)):
            brought[kind].append(along_y(part(weight, 3 - place), hop))
    far = [(jnp.concatenate(side, axis=1), jnp.concatenate([to_core(block) for block in side], axis=1)) for side in brought]

    normed = attend(tokens, attend_weight, output_weight, attend_gain, query_length)

    def feed(up, down):
        hidden = jax.nn.gelu(
            jnp.dot(normed, up, preferred_element_type=jnp.float32), approximate=False
        ).astype(jnp.bfloat16)
        return lax.dot_general(hidden, down, (((1,), (1,)), ((), ())), preferred_element_type=jnp.float32)

    reduced = feed(own[0][0], own[1][0]) + feed(own[0][1], own[1][1])
    reduced = reduced + feed(far[0][0], far[1][0]) + feed(far[0][1], far[1][1])
    layer_out = norm_rows(normed.astype(jnp.float32) + reduced, mlp_gain).astype(jnp.bfloat16)
    projected = jnp.dot(layer_out, embed_weight, preferred_element_type=jnp.float32)
    unit = projected * lax.rsqrt(jnp.sum(projected * projected, axis=-1, keepdims=True) + 1e-06)
    live_slot = jnp.arange(SEQ)[None, :] < query_length[:, None]
    embedded = jnp.where(live_slot.reshape(rows, 1), unit, 0.0).astype(jnp.bfloat16)

    lengths = lax.all_gather(document_length, "req", axis=0, tiled=True)
    limits = lengths[candidates]
    owner = candidates // held_docs
    parts = jnp.arange(mlp_size, dtype=jnp.int32)
    away_z = (z - owner // width) % DEPTH
    away_x = (x - owner % width) % width
    away_y = (y - parts // CORES) % tall
    away_core = (core + parts) % CORES
    spots = (away_core * DEPTH + away_z[..., None]) * width + away_x[..., None]
    spots = (spots * tall + away_y) * held_docs + (candidates % held_docs)[..., None]
    scores = score(embedded, pieces, spots.astype(jnp.int32), limits)
    return (embedded, scores)


def solution(mesh):
    return jax.shard_map(
        functools.partial(on_device, mesh.shape["req"], mesh.shape["mlp"]),
        mesh=mesh,
        in_specs=(
            P(("req", "mlp"), None),
            P(),
            P(),
            P(),
            P(None, "mlp"),
            P(None, "mlp"),
            P(),
            P(),
            P(("req", "mlp")),
            P("req", "mlp", None),
            P("req"),
            P(("req", "mlp"), None),
        ),
        out_specs=(P(("req", "mlp"), None), P(("req", "mlp"), None)),
        check_vma=False,
    )
```

```python
import functools

import jax
import jax.numpy as jnp
from jax import lax
from jax.experimental import pallas as pl
from jax.experimental.pallas import tpu as pltpu
from jax.sharding import PartitionSpec as P

D = 1024
HEADS = 16
HD = 64
P_SIZE = 128
SEQ = 128
CORES = 2
DEPTH = 4
MIB = 1024 * 1024


def norm_rows(values, scaling):
    average = jnp.mean(values, axis=-1, keepdims=True)
    centred = values - average
    variance = jnp.mean(centred * centred, axis=-1, keepdims=True)
    return centred * lax.rsqrt(variance + 1e-05) * scaling


def pack_kernel(tokens_ref, attend_ref, *refs):
    packed = refs[-1]
    wide = 512

    def project(step, carry):
        columns = pl.ds(pl.multiple_of(step * wide, wide), wide)
        packed[:, columns] = jnp.dot(
            tokens_ref[...], attend_ref[:, columns], preferred_element_type=jnp.float32
        ).astype(jnp.bfloat16)
        return carry

    lax.fori_loop(0, 3 * D // wide, project, 0)


def attend_kernel(length_ref, packed, tokens_ref, output_ref, gain_ref, *refs):
    normed_ref, context = refs[-2:]
    rows = tokens_ref.shape[0]
    lane = lax.broadcasted_iota(jnp.int32, (SEQ, 2 * HD), 1)
    low = lane < HD
    key_slot = lax.broadcasted_iota(jnp.int32, (2 * SEQ, SEQ), 1)

    def one_request(request, carry):
        here = pl.ds(pl.multiple_of(request * SEQ, SEQ), SEQ)
        live = key_slot < length_ref[request]
        for pair in range(HEADS // 2):
            at = pair * 2 * HD
            query = packed[here, at : at + 2 * HD]
            keys = packed[here, D + at : D + at + 2 * HD]
            value = packed[here, 2 * D + at : 2 * D + at + 2 * HD]
            none = jnp.zeros_like(query)
            both = jnp.concatenate([jnp.where(low, query, none), jnp.where(low, none, query)], axis=0)
            logits = lax.dot_general(
                both, keys, (((1,), (1,)), ((), ())), preferred_element_type=jnp.float32
            ) * HD ** (-0.5)
            logits = jnp.where(live, logits, -1e30)
            weights = jnp.exp(logits - jnp.max(logits, axis=-1, keepdims=True))
            probs = (weights / jnp.sum(weights, axis=-1, keepdims=True)).astype(jnp.bfloat16)
            mixed = jnp.dot(probs, value, preferred_element_type=jnp.float32)
            context[here, at : at + 2 * HD] = jnp.where(low, mixed[:SEQ], mixed[SEQ:]).astype(jnp.bfloat16)
        return carry

    lax.fori_loop(0, rows // SEQ, one_request, 0)

    def finish(step, carry):
        here = pl.ds(pl.multiple_of(step * SEQ, SEQ), SEQ)
        attended = jnp.dot(context[here, :], output_ref[...], preferred_element_type=jnp.float32)
        normed_ref[here, :] = norm_rows(
            tokens_ref[here, :].astype(jnp.float32) + attended, gain_ref[...]
        ).astype(jnp.bfloat16)
        return carry

    lax.fori_loop(0, rows // SEQ, finish, 0)


def gate(values, awaited):
    anywhere = pl.BlockSpec(memory_space=pl.ANY)
    return pl.pallas_call(
        lambda *refs: None,
        out_shape=[jax.ShapeDtypeStruct(value.shape, value.dtype) for value in values],
        in_specs=[anywhere] * (len(values) + len(awaited)),
        out_specs=[anywhere] * len(values),
        input_output_aliases={at: at for at in range(len(values))},
        compiler_params=pltpu.CompilerParams(vmem_limit_bytes=MIB),
        name="gate",
    )(*values, *awaited)


def pack(tokens, attend_weight, awaited):
    rows = tokens.shape[0]
    vmem, anywhere = pl.BlockSpec(memory_space=pltpu.VMEM), pl.BlockSpec(memory_space=pl.ANY)
    return pl.pallas_call(
        pack_kernel,
        out_shape=jax.ShapeDtypeStruct((rows, 3 * D), jnp.bfloat16),
        in_specs=[vmem] * 2 + [anywhere] * len(awaited),
        out_specs=vmem,
        compiler_params=pltpu.CompilerParams(vmem_limit_bytes=32 * MIB),
        cost_estimate=pl.CostEstimate(flops=rows * D * D * 6, bytes_accessed=10 * MIB, transcendentals=0),
        name="pack",
    )(tokens, attend_weight, *awaited)


def attend(packed, tokens, output_weight, attend_gain, query_length, awaited):
    rows = tokens.shape[0]
    vmem, anywhere = pl.BlockSpec(memory_space=pltpu.VMEM), pl.BlockSpec(memory_space=pl.ANY)
    return pl.pallas_call(
        attend_kernel,
        out_shape=jax.ShapeDtypeStruct((rows, D), jnp.bfloat16),
        in_specs=[pl.BlockSpec(memory_space=pltpu.SMEM)] + [vmem] * 4 + [anywhere] * len(awaited),
        out_specs=vmem,
        scratch_shapes=[pltpu.VMEM((rows, D), jnp.bfloat16)],
        compiler_params=pltpu.CompilerParams(vmem_limit_bytes=32 * MIB),
        cost_estimate=pl.CostEstimate(flops=rows * D * D * 6, bytes_accessed=8 * MIB, transcendentals=rows * SEQ * HEADS),
        name="attend",
    )(query_length, packed, tokens, output_weight, attend_gain.reshape(1, D), *awaited)


def feed_kernel(dims, last, awaited, carried, *refs):
    refs = list(refs)
    out_ref = refs.pop()
    refs = refs[: len(refs) - awaited]
    normed_ref = refs.pop(0)
    if last:
        length_ref, gain_ref, embed_ref = refs.pop(0), refs.pop(0), refs.pop(0)
    before = refs.pop(0) if carried else None
    step = 256
    total = None if before is None else before[...]
    pairs = []
    if dims == 2:
        for at in range(0, refs[0].shape[1], step):
            pairs.append((refs[0].at[:, at : at + step], refs[1].at[:, at : at + step]))
    else:
        for ref in refs:
            pairs.append((ref.at[0], ref.at[1]))
    for up, down in pairs:
        inner = jnp.dot(normed_ref[...], up[...], preferred_element_type=jnp.float32)
        hidden = (0.5 * inner * (1.0 + lax.erf(inner * 0.5**0.5))).astype(jnp.bfloat16)
        term = lax.dot_general(hidden, down[...], (((1,), (1,)), ((), ())), preferred_element_type=jnp.float32)
        total = term if total is None else total + term
    if not last:
        out_ref[...] = total
        return
    layer_out = norm_rows(normed_ref[...].astype(jnp.float32) + total, gain_ref[...]).astype(jnp.bfloat16)
    projected = jnp.dot(layer_out, embed_ref[...], preferred_element_type=jnp.float32)
    unit = projected * lax.rsqrt(jnp.sum(projected * projected, axis=-1, keepdims=True) + 1e-06)
    slot = lax.broadcasted_iota(jnp.int32, (SEQ, P_SIZE), 0)
    for request in range(unit.shape[0] // SEQ):
        block = unit[request * SEQ : (request + 1) * SEQ]
        out_ref[request * SEQ : (request + 1) * SEQ, :] = jnp.where(
            slot < length_ref[request], block, 0.0
        ).astype(jnp.bfloat16)


def feed(normed, weights, before=None, ending=None, awaited=()):
    rows = normed.shape[0]
    smem, vmem = pl.BlockSpec(memory_space=pltpu.SMEM), pl.BlockSpec(memory_space=pltpu.VMEM)
    args, specs = [normed], [vmem]
    if ending is not None:
        args += list(ending)
        specs += [smem, vmem, vmem]
    if before is not None:
        args.append(before)
        specs.append(vmem)
    args += weights
    specs += [vmem] * len(weights) + [pl.BlockSpec(memory_space=pl.ANY)] * len(awaited)
    if ending is None:
        shape = jax.ShapeDtypeStruct((rows, D), jnp.float32)
    else:
        shape = jax.ShapeDtypeStruct((rows, P_SIZE), jnp.bfloat16)
    units = sum(weight.size for weight in weights) // (2 * D)
    return pl.pallas_call(
        functools.partial(feed_kernel, weights[0].ndim, ending is not None, len(awaited), before is not None),
        out_shape=shape,
        in_specs=specs,
        out_specs=vmem,
        compiler_params=pltpu.CompilerParams(vmem_limit_bytes=40 * MIB),
        cost_estimate=pl.CostEstimate(flops=4 * rows * D * units, bytes_accessed=8 * MIB, transcendentals=rows * units),
        name="feed",
    )(*args, *awaited)


def score_kernel(spots_ref, marks_ref, rows_ref, embedded_ref, pieces_ref, best_ref):
    requests, picks, parts = spots_ref.shape
    piece_rows = pieces_ref.shape[1]
    position = lax.broadcasted_iota(jnp.int32, (parts * piece_rows, SEQ), 0).astype(jnp.float32)
    row = lax.broadcasted_iota(jnp.int32, (piece_rows, P_SIZE), 0)

    def one_request(request, carry):
        block = embedded_ref[pl.ds(pl.multiple_of(request * SEQ, SEQ), SEQ), :]
        found = []
        for pick in range(picks):
            chosen = jnp.concatenate([pieces_ref[spots_ref[request, pick, part]] for part in range(parts)], axis=0)
            listed = pieces_ref[marks_ref[request, pick]].astype(jnp.float32)
            limit = jnp.sum(jnp.where(row == rows_ref[request, pick], listed, 0.0), axis=0, keepdims=True)
            sims = lax.dot_general(
                chosen, block, (((1,), (1,)), ((), ())), preferred_element_type=jnp.float32
            )
            sims = jnp.where(position < limit, sims, -1e30)
            found.append(jnp.max(sims, axis=0, keepdims=True))
        best_ref[request] = jnp.concatenate(found, axis=0)
        return carry

    lax.fori_loop(0, requests, one_request, 0)


def score(embedded, pieces, spots, marks, rows):
    requests, picks, parts = spots.shape
    smem, vmem = pl.BlockSpec(memory_space=pltpu.SMEM), pl.BlockSpec(memory_space=pltpu.VMEM)
    best = pl.pallas_call(
        score_kernel,
        out_shape=jax.ShapeDtypeStruct((requests, picks, SEQ), jnp.float32),
        in_specs=[smem, smem, smem, vmem, vmem],
        out_specs=vmem,
        compiler_params=pltpu.CompilerParams(vmem_limit_bytes=32 * MIB),
        cost_estimate=pl.CostEstimate(flops=2 * requests * picks * 256 * SEQ * P_SIZE, bytes_accessed=5 * MIB, transcendentals=0),
        name="score",
    )(spots, marks, rows, embedded, pieces)
    return jnp.sum(best, axis=2)


def on_device(
    req_size,
    mlp_size,
    tokens,
    attend_weight,
    output_weight,
    attend_gain,
    up_weight,
    down_weight,
    mlp_gain,
    embed_weight,
    query_length,
    documents,
    document_length,
    candidates,
):
    rows = tokens.shape[0]
    held_docs, shard_rows = documents.shape[:2]
    width, tall = req_size // DEPTH, mlp_size // CORES
    req, mlp = lax.axis_index("req"), lax.axis_index("mlp")
    z, x, y, core = req // width, req % width, mlp // CORES, mlp % CORES

    def to_core(block):
        return lax.ppermute(block, "mlp", [(m, m ^ 1) for m in range(mlp_size)])

    def along_y(block, hops):
        return lax.ppermute(block, "mlp", [(m, (m + CORES * hops) % mlp_size) for m in range(mlp_size)])

    def along_x(block, hops):
        return lax.ppermute(
            block, "req", [(r, r // width * width + (r % width + hops) % width) for r in range(req_size)]
        )

    def to_pair(block, stride):
        return lax.ppermute(block, "req", [(r, r ^ stride) for r in range(req_size)])

    listed = jnp.zeros((shard_rows, P_SIZE), jnp.bfloat16)
    listed = listed.at[:held_docs].set(document_length.astype(jnp.bfloat16)[:, None])
    block = jnp.concatenate([documents, listed[None]], axis=0)
    held = held_docs + 1
    upward, downward = [block], [block]
    for _ in range(1, DEPTH):
        upward.append(lax.ppermute(upward[-1], "req", [(r, r + width) for r in range(req_size - width)]))
        downward.append(lax.ppermute(downward[-1], "req", [(r, r - width) for r in range(width, req_size)]))
    around = jnp.stack(
        [block] + [jnp.where(z >= hop, upward[hop], downward[DEPTH - hop]) for hop in range(1, DEPTH)]
    )
    from_x = [along_x(around, hop) for hop in range(1, width)]

    place = x % 2 + 2 * (z % 2)
    part_columns = up_weight.shape[1] // 4

    def part(which):
        return jnp.stack(
            [lax.dynamic_slice_in_dim(w, which * part_columns, part_columns, 1) for w in (up_weight, down_weight)]
        )

    near = part(place)
    firsts = [along_y(near, hop) for hop in range(1, tall)]
    partner = [to_core(up_weight), to_core(down_weight)]


    packed = pack(tokens, attend_weight, [])
    normed = attend(packed, tokens, output_weight, attend_gain, query_length, [])
    around = jnp.stack([around] + from_x)
    held_back = gate([around] + firsts, [normed])
    around, firsts = held_back[0], held_back[1:]
    total = feed(normed, [up_weight, down_weight])
    total = feed(normed, partner, total)
    quarters = []
    for first in firsts:
        quarters += [first, to_pair(first, 1), to_pair(first, width)]
    around = jnp.stack([around] + [along_y(around, hop) for hop in range(1, tall)])
    quarters = gate(quarters, [total])
    halves = []
    for at in range(0, len(quarters), 3):
        halves.append(to_pair(quarters[at + 1][:, :, : part_columns // 2], width))
        halves.append(to_pair(quarters[at + 2][:, :, part_columns // 2 :], 1))
    passed = [to_core(quarter) for quarter in quarters]
    for at in range(0, len(quarters), 3):
        total = feed(normed, quarters[at : at + 3], total)
        total = feed(normed, passed[at : at + 3], total)
    held_back = gate([around] + halves, [total])
    around, halves = held_back[0], held_back[1:]
    pieces = jnp.stack([around, to_core(around)]).reshape(-1, shard_rows, P_SIZE)
    passed = [to_core(half) for half in halves]
    total = feed(normed, halves, total)
    ending = (query_length, mlp_gain.reshape(1, D), embed_weight)
    embedded = feed(normed, passed, total, ending)

    owner = candidates // held_docs
    parts = jnp.arange(mlp_size, dtype=jnp.int32)
    away_z = (z - owner // width) % DEPTH
    away_x = (x - owner % width) % width
    away_y = (y - parts // CORES) % tall
    away_core = (core + parts) % CORES
    spots = (away_core * tall + away_y) * width + away_x[..., None]
    spots = ((spots * DEPTH + away_z[..., None]) * held).astype(jnp.int32)
    places = (candidates % held_docs).astype(jnp.int32)
    scores = score(embedded, pieces, spots + places[..., None], spots[..., 0] + held_docs, places)
    return (embedded, scores)


def solution(mesh):
    return jax.shard_map(
        functools.partial(on_device, mesh.shape["req"], mesh.shape["mlp"]),
        mesh=mesh,
        in_specs=(
            P(("req", "mlp"), None),
            P(),
            P(),
            P(),
            P(None, "mlp"),
            P(None, "mlp"),
            P(),
            P(),
            P(("req", "mlp")),
            P("req", "mlp", None),
            P("req"),
            P(("req", "mlp"), None),
        ),
        out_specs=(P(("req", "mlp"), None), P(("req", "mlp"), None)),
        check_vma=False,
    )
```

```python
import functools

import jax
import jax.numpy as jnp
from jax import lax
from jax.experimental import pallas as pl
from jax.experimental.pallas import tpu as pltpu
from jax.sharding import PartitionSpec as P

D = 1024
HEADS = 16
HD = 64
P_SIZE = 128
SEQ = 128
CORES = 2
DEPTH = 4
MIB = 1024 * 1024


def norm_rows(values, scaling):
    average = jnp.mean(values, axis=-1, keepdims=True)
    centred = values - average
    variance = jnp.mean(centred * centred, axis=-1, keepdims=True)
    return centred * lax.rsqrt(variance + 1e-05) * scaling


def pack_kernel(tokens_ref, attend_ref, *refs):
    packed = refs[-1]
    wide = 512

    def project(step, carry):
        columns = pl.ds(pl.multiple_of(step * wide, wide), wide)
        packed[:, columns] = jnp.dot(
            tokens_ref[...], attend_ref[:, columns], preferred_element_type=jnp.float32
        ).astype(jnp.bfloat16)
        return carry

    lax.fori_loop(0, 3 * D // wide, project, 0)


def attend_kernel(length_ref, packed, tokens_ref, output_ref, gain_ref, *refs):
    normed_ref, context = refs[-2:]
    rows = tokens_ref.shape[0]
    lane = lax.broadcasted_iota(jnp.int32, (SEQ, 2 * HD), 1)
    low = lane < HD
    key_slot = lax.broadcasted_iota(jnp.int32, (2 * SEQ, SEQ), 1)

    def one_request(request, carry):
        here = pl.ds(pl.multiple_of(request * SEQ, SEQ), SEQ)
        live = key_slot < length_ref[request]
        for pair in range(HEADS // 2):
            at = pair * 2 * HD
            query = packed[here, at : at + 2 * HD]
            keys = packed[here, D + at : D + at + 2 * HD]
            value = packed[here, 2 * D + at : 2 * D + at + 2 * HD]
            none = jnp.zeros_like(query)
            both = jnp.concatenate([jnp.where(low, query, none), jnp.where(low, none, query)], axis=0)
            logits = lax.dot_general(
                both, keys, (((1,), (1,)), ((), ())), preferred_element_type=jnp.float32
            ) * HD ** (-0.5)
            logits = jnp.where(live, logits, -1e30)
            weights = jnp.exp(logits - jnp.max(logits, axis=-1, keepdims=True))
            probs = (weights / jnp.sum(weights, axis=-1, keepdims=True)).astype(jnp.bfloat16)
            mixed = jnp.dot(probs, value, preferred_element_type=jnp.float32)
            context[here, at : at + 2 * HD] = jnp.where(low, mixed[:SEQ], mixed[SEQ:]).astype(jnp.bfloat16)
        return carry

    lax.fori_loop(0, rows // SEQ, one_request, 0)

    def finish(step, carry):
        here = pl.ds(pl.multiple_of(step * SEQ, SEQ), SEQ)
        attended = jnp.dot(context[here, :], output_ref[...], preferred_element_type=jnp.float32)
        normed_ref[here, :] = norm_rows(
            tokens_ref[here, :].astype(jnp.float32) + attended, gain_ref[...]
        ).astype(jnp.bfloat16)
        return carry

    lax.fori_loop(0, rows // SEQ, finish, 0)


def gate(values, awaited):
    anywhere = pl.BlockSpec(memory_space=pl.ANY)
    return pl.pallas_call(
        lambda *refs: None,
        out_shape=[jax.ShapeDtypeStruct(value.shape, value.dtype) for value in values],
        in_specs=[anywhere] * (len(values) + len(awaited)),
        out_specs=[anywhere] * len(values),
        input_output_aliases={at: at for at in range(len(values))},
        compiler_params=pltpu.CompilerParams(vmem_limit_bytes=MIB),
        name="gate",
    )(*values, *awaited)


def pack(tokens, attend_weight, awaited):
    rows = tokens.shape[0]
    vmem, anywhere = pl.BlockSpec(memory_space=pltpu.VMEM), pl.BlockSpec(memory_space=pl.ANY)
    return pl.pallas_call(
        pack_kernel,
        out_shape=jax.ShapeDtypeStruct((rows, 3 * D), jnp.bfloat16),
        in_specs=[vmem] * 2 + [anywhere] * len(awaited),
        out_specs=vmem,
        compiler_params=pltpu.CompilerParams(vmem_limit_bytes=32 * MIB),
        cost_estimate=pl.CostEstimate(flops=rows * D * D * 6, bytes_accessed=10 * MIB, transcendentals=0),
        name="pack",
    )(tokens, attend_weight, *awaited)


def attend(packed, tokens, output_weight, attend_gain, query_length, awaited):
    rows = tokens.shape[0]
    vmem, anywhere = pl.BlockSpec(memory_space=pltpu.VMEM), pl.BlockSpec(memory_space=pl.ANY)
    return pl.pallas_call(
        attend_kernel,
        out_shape=jax.ShapeDtypeStruct((rows, D), jnp.bfloat16),
        in_specs=[pl.BlockSpec(memory_space=pltpu.SMEM)] + [vmem] * 4 + [anywhere] * len(awaited),
        out_specs=vmem,
        scratch_shapes=[pltpu.VMEM((rows, D), jnp.bfloat16)],
        compiler_params=pltpu.CompilerParams(vmem_limit_bytes=32 * MIB),
        cost_estimate=pl.CostEstimate(flops=rows * D * D * 6, bytes_accessed=8 * MIB, transcendentals=rows * SEQ * HEADS),
        name="attend",
    )(query_length, packed, tokens, output_weight, attend_gain.reshape(1, D), *awaited)


def feed_kernel(dims, last, awaited, carried, *refs):
    refs = list(refs)
    out_ref = refs.pop()
    refs = refs[: len(refs) - awaited]
    normed_ref = refs.pop(0)
    if last:
        length_ref, gain_ref, embed_ref = refs.pop(0), refs.pop(0), refs.pop(0)
    before = refs.pop(0) if carried else None
    step = 256
    total = None if before is None else before[...]
    pairs = []
    if dims == 2:
        for at in range(0, refs[0].shape[1], step):
            pairs.append((refs[0].at[:, at : at + step], refs[1].at[:, at : at + step]))
    else:
        for ref in refs:
            pairs.append((ref.at[0], ref.at[1]))
    for up, down in pairs:
        inner = jnp.dot(normed_ref[...], up[...], preferred_element_type=jnp.float32)
        hidden = (0.5 * inner * (1.0 + lax.erf(inner * 0.5**0.5))).astype(jnp.bfloat16)
        term = lax.dot_general(hidden, down[...], (((1,), (1,)), ((), ())), preferred_element_type=jnp.float32)
        total = term if total is None else total + term
    if not last:
        out_ref[...] = total
        return
    layer_out = norm_rows(normed_ref[...].astype(jnp.float32) + total, gain_ref[...]).astype(jnp.bfloat16)
    projected = jnp.dot(layer_out, embed_ref[...], preferred_element_type=jnp.float32)
    unit = projected * lax.rsqrt(jnp.sum(projected * projected, axis=-1, keepdims=True) + 1e-06)
    slot = lax.broadcasted_iota(jnp.int32, (SEQ, P_SIZE), 0)
    for request in range(unit.shape[0] // SEQ):
        block = unit[request * SEQ : (request + 1) * SEQ]
        out_ref[request * SEQ : (request + 1) * SEQ, :] = jnp.where(
            slot < length_ref[request], block, 0.0
        ).astype(jnp.bfloat16)


def feed(normed, weights, before=None, ending=None, awaited=()):
    rows = normed.shape[0]
    smem, vmem = pl.BlockSpec(memory_space=pltpu.SMEM), pl.BlockSpec(memory_space=pltpu.VMEM)
    args, specs = [normed], [vmem]
    if ending is not None:
        args += list(ending)
        specs += [smem, vmem, vmem]
    if before is not None:
        args.append(before)
        specs.append(vmem)
    args += weights
    specs += [vmem] * len(weights) + [pl.BlockSpec(memory_space=pl.ANY)] * len(awaited)
    if ending is None:
        shape = jax.ShapeDtypeStruct((rows, D), jnp.float32)
    else:
        shape = jax.ShapeDtypeStruct((rows, P_SIZE), jnp.bfloat16)
    units = sum(weight.size for weight in weights) // (2 * D)
    return pl.pallas_call(
        functools.partial(feed_kernel, weights[0].ndim, ending is not None, len(awaited), before is not None),
        out_shape=shape,
        in_specs=specs,
        out_specs=vmem,
        compiler_params=pltpu.CompilerParams(vmem_limit_bytes=40 * MIB),
        cost_estimate=pl.CostEstimate(flops=4 * rows * D * units, bytes_accessed=8 * MIB, transcendentals=rows * units),
        name="feed",
    )(*args, *awaited)


def score_kernel(spots_ref, marks_ref, rows_ref, embedded_ref, pieces_ref, best_ref):
    requests, picks, parts = spots_ref.shape
    piece_rows = pieces_ref.shape[1]
    position = lax.broadcasted_iota(jnp.int32, (parts * piece_rows, SEQ), 0).astype(jnp.float32)
    row = lax.broadcasted_iota(jnp.int32, (piece_rows, P_SIZE), 0)

    def one_request(request, carry):
        block = embedded_ref[pl.ds(pl.multiple_of(request * SEQ, SEQ), SEQ), :]
        found = []
        for pick in range(picks):
            chosen = jnp.concatenate([pieces_ref[spots_ref[request, pick, part]] for part in range(parts)], axis=0)
            listed = pieces_ref[marks_ref[request, pick]].astype(jnp.float32)
            limit = jnp.sum(jnp.where(row == rows_ref[request, pick], listed, 0.0), axis=0, keepdims=True)
            sims = lax.dot_general(
                chosen, block, (((1,), (1,)), ((), ())), preferred_element_type=jnp.float32
            )
            sims = jnp.where(position < limit, sims, -1e30)
            found.append(jnp.max(sims, axis=0, keepdims=True))
        best_ref[request] = jnp.concatenate(found, axis=0)
        return carry

    lax.fori_loop(0, requests, one_request, 0)


def score(embedded, pieces, spots, marks, rows):
    requests, picks, parts = spots.shape
    smem, vmem = pl.BlockSpec(memory_space=pltpu.SMEM), pl.BlockSpec(memory_space=pltpu.VMEM)
    best = pl.pallas_call(
        score_kernel,
        out_shape=jax.ShapeDtypeStruct((requests, picks, SEQ), jnp.float32),
        in_specs=[smem, smem, smem, vmem, vmem],
        out_specs=vmem,
        compiler_params=pltpu.CompilerParams(vmem_limit_bytes=32 * MIB),
        cost_estimate=pl.CostEstimate(flops=2 * requests * picks * 256 * SEQ * P_SIZE, bytes_accessed=5 * MIB, transcendentals=0),
        name="score",
    )(spots, marks, rows, embedded, pieces)
    return jnp.sum(best, axis=2)


def on_device(
    req_size,
    mlp_size,
    tokens,
    attend_weight,
    output_weight,
    attend_gain,
    up_weight,
    down_weight,
    mlp_gain,
    embed_weight,
    query_length,
    documents,
    document_length,
    candidates,
):
    rows = tokens.shape[0]
    held_docs, shard_rows = documents.shape[:2]
    width, tall = req_size // DEPTH, mlp_size // CORES
    req, mlp = lax.axis_index("req"), lax.axis_index("mlp")
    z, x, y, core = req // width, req % width, mlp // CORES, mlp % CORES

    def to_core(block):
        return lax.ppermute(block, "mlp", [(m, m ^ 1) for m in range(mlp_size)])

    def along_y(block, hops):
        return lax.ppermute(block, "mlp", [(m, (m + CORES * hops) % mlp_size) for m in range(mlp_size)])

    def along_x(block, hops):
        return lax.ppermute(
            block, "req", [(r, r // width * width + (r % width + hops) % width) for r in range(req_size)]
        )

    def to_pair(block, stride):
        return lax.ppermute(block, "req", [(r, r ^ stride) for r in range(req_size)])

    listed = jnp.zeros((shard_rows, P_SIZE), jnp.bfloat16)
    listed = listed.at[:held_docs].set(document_length.astype(jnp.bfloat16)[:, None])
    block = jnp.concatenate([documents, listed[None]], axis=0)
    held = held_docs + 1
    around = jnp.stack([block, to_pair(block, width)])
    around = jnp.stack([around, to_pair(around, 2 * width)]).reshape(DEPTH, *block.shape)
    packed = pack(tokens, attend_weight, [])
    around = gate([around], [packed])[0]
    from_x = [along_x(around, hop) for hop in range(1, width)]

    place = x % 2 + 2 * (z % 2)
    part_columns = up_weight.shape[1] // 4

    def part(which):
        return jnp.stack(
            [lax.dynamic_slice_in_dim(w, which * part_columns, part_columns, 1) for w in (up_weight, down_weight)]
        )

    near = part(place)
    firsts = [along_y(near, hop) for hop in range(1, tall)]
    partner = [to_core(up_weight), to_core(down_weight)]


    normed = attend(packed, tokens, output_weight, attend_gain, query_length, [])
    around = jnp.stack([around] + from_x)
    held_back = gate([around] + firsts, [normed])
    around, firsts = held_back[0], held_back[1:]
    total = feed(normed, [up_weight, down_weight])
    total = feed(normed, partner, total)
    quarters = []
    for first in firsts:
        quarters += [first, to_pair(first, 1), to_pair(first, width)]
    around = jnp.stack([around] + [along_y(around, hop) for hop in range(1, tall)])
    quarters = gate(quarters, [total])
    halves = []
    for at in range(0, len(quarters), 3):
        halves.append(to_pair(quarters[at + 1][:, :, : part_columns // 2], width))
        halves.append(to_pair(quarters[at + 2][:, :, part_columns // 2 :], 1))
    passed = [to_core(quarter) for quarter in quarters]
    for at in range(0, len(quarters), 3):
        total = feed(normed, quarters[at : at + 3], total)
        total = feed(normed, passed[at : at + 3], total)
    held_back = gate([around] + halves, [total])
    around, halves = held_back[0], held_back[1:]
    pieces = jnp.stack([around, to_core(around)]).reshape(-1, shard_rows, P_SIZE)
    passed = [to_core(half) for half in halves]
    total = feed(normed, halves, total)
    ending = (query_length, mlp_gain.reshape(1, D), embed_weight)
    embedded = feed(normed, passed, total, ending)

    owner = candidates // held_docs
    parts = jnp.arange(mlp_size, dtype=jnp.int32)
    away_z = z ^ (owner // width)
    away_x = (x - owner % width) % width
    away_y = (y - parts // CORES) % tall
    away_core = (core + parts) % CORES
    spots = (away_core * tall + away_y) * width + away_x[..., None]
    spots = ((spots * DEPTH + away_z[..., None]) * held).astype(jnp.int32)
    places = (candidates % held_docs).astype(jnp.int32)
    scores = score(embedded, pieces, spots + places[..., None], spots[..., 0] + held_docs, places)
    return (embedded, scores)


def solution(mesh):
    return jax.shard_map(
        functools.partial(on_device, mesh.shape["req"], mesh.shape["mlp"]),
        mesh=mesh,
        in_specs=(
            P(("req", "mlp"), None),
            P(),
            P(),
            P(),
            P(None, "mlp"),
            P(None, "mlp"),
            P(),
            P(),
            P(("req", "mlp")),
            P("req", "mlp", None),
            P("req"),
            P(("req", "mlp"), None),
        ),
        out_specs=(P(("req", "mlp"), None), P(("req", "mlp"), None)),
        check_vma=False,
    )
```
